512 devices in a mesh: dp: 8 (over y, core), tile: 64 (over x, z).
Axes of the slice: x: 4, y: 4, z: 16, core: 2. Of those that a mesh axis runs over, the one named last changes fastest.
Arguments:
- tokens: bfloat16 [65536, 2048], P(('dp', 'tile')), may hold values from -6 to 6
- expert_ids: int32 [65536, 8], P(('dp', 'tile')), may hold values from 0 to 127, all different within a row; in each aligned block of 128 rows (0 to 127, 128 to 255, ...) at most 10 rows name the same one
- gates: float32 [65536, 8], P(('dp', 'tile')), may hold values from 0.05 to 1
- tile_slot: int32 [60], replicated, may hold values from 0 to 63, as said below
- w_gate: bfloat16 [64, 2048, 128], P('tile'), may hold values from -0.125 to 0.125
- w_up: bfloat16 [64, 2048, 128], P('tile'), may hold values from -0.125 to 0.125
- w_down: bfloat16 [64, 128, 2048], P('tile'), may hold values from -0.21875 to 0.21875
- grad_out: bfloat16 [65536, 2048], P(('dp', 'tile')), may hold values from -6 to 6
Outputs:
- layer_out: bfloat16 [65536, 2048], P(('dp', 'tile'))
- token_grads: bfloat16 [65536, 2048], P(('dp', 'tile'))
- gate_grads: float32 [65536, 8], P(('dp', 'tile'))
- gate_weight_grads: bfloat16 [64, 2048, 128], P('tile', 'dp')
- up_weight_grads: bfloat16 [64, 2048, 128], P('tile', 'dp')
- down_weight_grads: bfloat16 [64, 128, 2048], P('tile', None, 'dp')
The draws below stay inside these ranges and needn't reach their ends.
Inputs may be any that keep to these rules, and one draw needn't show every extreme that they name: `expert_ids`: each row names 8 different experts; the 128 rows of one device name one expert at most 10 times. `tile_slot`: all entries differ.
All inputs are finite; a program needn't handle non-finite values.
Results may differ from the reference program's by a relative error of at most 0.017.
Values may be sent and summed in bfloat16 or wider, within the bound.
No kernel may reach another device: no remote copies, remote signals or barrier semaphores. Data moves between devices by JAX's collectives and lax.ppermute only.
A program may use at most 64 MiB of HBM per device.

```python
import math
import jax
import jax.numpy as jnp
import numpy as np
from jax import lax

D = 2048
EXP_HIDDEN = 768
EXPERTS = 128
TOPK = 8
TILE_W = 128
TOK_DEV = 128
HTILES = 6
WIN_EXP = 10
TILES = 60
CAP = 10
TOKENS = 65536
N_DP = 8
N_TILE = 64


def draw_tile_slot(key, part):
    key = jax.random.fold_in(key, 11)
    shuffled = jax.random.permutation(key, jnp.arange(N_TILE, dtype=jnp.int32))
    return shuffled[:TILES].astype(jnp.int32)


def levels(own_key, extent, cuts, low, top_value):
    loudness, own = 1.0, jax.random.fold_in(own_key, 6)
    for axis_at, parts in cuts:
        heights = jnp.exp(jax.random.uniform(jax.random.fold_in(own, axis_at), (parts,), jnp.float32, low / len(cuts), top_value / len(cuts)))
        loudness = loudness * jnp.repeat(heights, extent[axis_at] // parts).reshape([-1 if axis == axis_at else 1 for axis in range(len(extent))])
    return loudness


def routed_block(stream_key, own, number, rows, number_of, top, most, skew):
    sequence = jax.random.permutation(stream_key, number_of)
    packed, common = portions_of(number_of, rows * top, most, skew, True), portions_of(number_of, rows * top, most, skew, False)
    places = jnp.arange(number_of)

    def named(sizes, offset_by):
        used = int((sizes > 0).sum())
        fixed = max(1, used // 4)
        passed = fixed + (places - fixed + offset_by * (used - fixed)) % max(1, number_of - fixed)
        return jnp.zeros((number_of,), jnp.int32).at[sequence[jnp.where(places < fixed, places, passed)]].set(jnp.asarray(sizes, jnp.int32))

    sizes = jnp.where(number % 4 == 0, named(packed, number // 4), named(common, number - number // 4 - 1))
    mixed = jax.random.permutation(jax.random.fold_in(own, 3), number_of)
    donor, taker = mixed[0:number_of // 2 * 2:2], mixed[1:number_of // 2 * 2:2]
    margin = jnp.minimum(sizes[donor] - 1, most - sizes[taker]) // 2
    margin = jnp.where((donor == sequence[0]) | (taker == sequence[0]) | (sizes[taker] == 0), 0, jnp.maximum(margin, 0))
    passed = jax.random.randint(jax.random.fold_in(own, 4), (number_of // 2,), 0, 1 << 20) % (margin + 1)
    sizes = sizes.at[donor].add(-passed).at[taker].add(passed)
    members = jnp.searchsorted(jnp.cumsum(sizes), jnp.arange(rows * top), side="right").astype(jnp.int32)
    grid = members.reshape(top, rows).T
    grid = grid[jax.random.permutation(jax.random.fold_in(own, 1), rows)]
    offset_by = jax.random.randint(jax.random.fold_in(own, 2), (rows, 1), 0, top)
    return jnp.take_along_axis(grid, (jnp.arange(top)[None, :] + offset_by) % top, axis=1)


def portions_of(count, total, most, lean, full):
    portions = [(1 << 20) // math.isqrt(grade ** lean) + 1 for grade in range(1, count + 1)]
    largest = most if full else min(most, max(-(-total // count), total * portions[0] // sum(portions)))
    least = 1 if total - largest >= count - 1 else 0
    holding, surplus = [largest] + [least] * (count - 1), total - largest - least * (count - 1)
    while surplus > 0:
        candidates = [i for i in range(1, count) if holding[i] < largest] or [i for i in range(1, count) if holding[i] < most]
        pool, left = sum([portions[i] for i in candidates]), surplus
        for i in candidates:
            extra = min(most - holding[i], max(1, left * portions[i] // pool), surplus)
            holding[i] = holding[i] + extra
            surplus = surplus - extra
    return np.array(holding)


def bell_draw(rng, extent, width, reach, shards=(), kind=jnp.bfloat16):
    level = levels(rng, extent, shards, -0.22, 0.18) if shards else 1.0
    result = jax.random.normal(rng, extent, jnp.float32) * width * level
    return jnp.minimum(jnp.maximum(result, -reach), reach).astype(kind)


def setup_inputs(seed: int = 0) -> dict:
    key_of = jax.random.split(jax.random.key(seed), 9)
    tokens = bell_draw(key_of[0], (TOKENS, D), 1.0, 6.0, ((0, 512),))
    expert_ids_keys = jax.random.split(jax.random.fold_in(key_of[1], 1), TOKENS // TOK_DEV)
    expert_ids_turns = jax.random.permutation(jax.random.fold_in(key_of[1], 3), TOKENS // TOK_DEV)
    expert_ids = jax.vmap(lambda own, number: routed_block(jax.random.fold_in(key_of[1], 2), own, number, TOK_DEV, EXPERTS, TOPK, CAP, 1))(expert_ids_keys, expert_ids_turns).reshape((TOKENS, TOPK))
    gates = jnp.clip(jnp.exp(math.log(1.0) - 2.9957323 * jax.random.uniform(key_of[2], (TOKENS, TOPK), jnp.float32) ** levels(key_of[2], (TOKENS, TOPK), ((0, 512),), -0.2, 0.2)), 0.05, 1.0)
    tile_slot = draw_tile_slot(jax.random.fold_in(key_of[8], 71), 0)
    w_gate = bell_draw(key_of[4], (N_TILE, D, TILE_W), D ** -0.5, 0.125, ((0, 64),))
    w_up = bell_draw(key_of[5], (N_TILE, D, TILE_W), D ** -0.5, 0.125, ((0, 64),))
    w_down = bell_draw(key_of[6], (N_TILE, TILE_W, D), EXP_HIDDEN ** -0.5, 0.21875, ((0, 64),))
    grad_out = bell_draw(key_of[7], (TOKENS, D), 1.0, 6.0, ((0, 512),))
    return {"tokens": tokens, "expert_ids": expert_ids, "gates": gates, "tile_slot": tile_slot, "w_gate": w_gate, "w_up": w_up, "w_down": w_down, "grad_out": grad_out}


def rounded(value):
    return lax.optimization_barrier(value.astype(jnp.bfloat16)).astype(jnp.float32)


def grouped_product(left, right):
    left_groups = left.reshape(N_DP, -1, left.shape[1]).astype(jnp.float32)
    right_groups = right.reshape(N_DP, -1, right.shape[1]).astype(jnp.float32)
    partial_sums = jnp.einsum("gmk,gmd->gkd", left_groups, right_groups)
    return jnp.sum(rounded(partial_sums), axis=0).astype(jnp.bfloat16)


def reference(tokens, expert_ids, gates, tile_slot, w_gate, w_up, w_down, grad_out):
    devices = N_DP * N_TILE
    per_device = TOK_DEV * TOPK
    rows_total = WIN_EXP * devices * CAP
    routes = expert_ids.reshape(devices, per_device)
    member = (routes[:, :, None] == jnp.arange(WIN_EXP, dtype=jnp.int32)[None, None, :]).astype(jnp.int32)
    earlier = jnp.cumsum(member, axis=1) - member
    slot_rank = jnp.sum(earlier * member, axis=2)
    device_index = jnp.arange(devices, dtype=jnp.int32)[:, None]
    route_index = jnp.arange(per_device, dtype=jnp.int32)[None, :]
    position = jnp.where(routes < WIN_EXP, (routes * devices + device_index) * CAP + slot_rank, rows_total)
    position = position.reshape(-1).astype(jnp.int32)
    token_index = (device_index * TOK_DEV + route_index // TOPK).reshape(-1).astype(jnp.int32)
    assign_index = (device_index * per_device + route_index).reshape(-1).astype(jnp.int32)
    slot_token = jnp.full((rows_total,), TOKENS, jnp.int32).at[position].set(token_index, mode="drop")
    slot_assign = jnp.full((rows_total,), TOKENS * TOPK, jnp.int32).at[position].set(assign_index, mode="drop")
    slot_gate = jnp.zeros((rows_total,), jnp.float32).at[position].set(gates.reshape(-1).astype(jnp.float32), mode="drop")
    slot_token = slot_token.reshape(WIN_EXP, devices * CAP)
    slot_assign = slot_assign.reshape(WIN_EXP, devices * CAP)
    slot_gate = slot_gate.reshape(WIN_EXP, devices * CAP)
    padded_tokens = jnp.concatenate([tokens, jnp.zeros((1, D), tokens.dtype)], axis=0)
    padded_grad = jnp.concatenate([grad_out, jnp.zeros((1, D), grad_out.dtype)], axis=0)

    def expert_step(carry, expert):
        out_acc, input_acc, gate_acc = carry
        token_rows = slot_token[expert]
        inputs = padded_tokens[token_rows]
        upstream = padded_grad[token_rows].astype(jnp.float32)
        gate_rows = slot_gate[expert]
        scaled = (gate_rows[:, None] * upstream).astype(jnp.bfloat16)
        expert_out = jnp.zeros((inputs.shape[0], D), jnp.float32)
        input_grad = jnp.zeros((inputs.shape[0], D), jnp.float32)
        gate_list = []
        up_list = []
        down_list = []
        for piece in range(HTILES):
            owner = tile_slot[expert * HTILES + piece]
            weight_gate = w_gate[owner]
            weight_up = w_up[owner]
            weight_down = w_down[owner]
            pre_gate = jnp.dot(inputs, weight_gate, preferred_element_type=jnp.float32)
            pre_up = jnp.dot(inputs, weight_up, preferred_element_type=jnp.float32)
            sigmoid_gate = jax.nn.sigmoid(pre_gate)
            activated = pre_gate * sigmoid_gate
            hidden = (activated * pre_up).astype(jnp.bfloat16)
            expert_out = expert_out + rounded(jnp.dot(hidden, weight_down, preferred_element_type=jnp.float32))
            hidden_grad = jnp.dot(scaled, weight_down.T, preferred_element_type=jnp.float32)
            up_pre_grad = (hidden_grad * activated).astype(jnp.bfloat16)
            gate_pre_grad = (hidden_grad * pre_up * sigmoid_gate * (1.0 + pre_gate * (1.0 - sigmoid_gate))).astype(jnp.bfloat16)
            tile_in = jnp.dot(gate_pre_grad, weight_gate.T, preferred_element_type=jnp.float32)
            tile_in = tile_in + jnp.dot(up_pre_grad, weight_up.T, preferred_element_type=jnp.float32)
            input_grad = input_grad + rounded(tile_in)
            gate_list.append(grouped_product(inputs, gate_pre_grad))
            up_list.append(grouped_product(inputs, up_pre_grad))
            down_list.append(grouped_product(hidden, scaled))
        gate_terms = jnp.sum(expert_out * upstream, axis=1)
        out_acc = out_acc.at[token_rows].add(gate_rows[:, None] * expert_out)
        input_acc = input_acc.at[token_rows].add(input_grad)
        gate_acc = gate_acc.at[slot_assign[expert]].add(gate_terms)
        return (out_acc, input_acc, gate_acc), (jnp.stack(gate_list), jnp.stack(up_list), jnp.stack(down_list))

    start = (jnp.zeros((TOKENS + 1, D), jnp.float32), jnp.zeros((TOKENS + 1, D), jnp.float32),
             jnp.zeros((TOKENS * TOPK + 1,), jnp.float32))
    carry, stacked = lax.scan(expert_step, start, jnp.arange(WIN_EXP, dtype=jnp.int32))
    out_acc, input_acc, gate_acc = carry
    gate_tiles, up_tiles, down_tiles = stacked
    gate_weight_grads = jnp.zeros((N_TILE, D, TILE_W), jnp.bfloat16).at[tile_slot].set(gate_tiles.reshape(TILES, D, TILE_W))
    up_weight_grads = jnp.zeros((N_TILE, D, TILE_W), jnp.bfloat16).at[tile_slot].set(up_tiles.reshape(TILES, D, TILE_W))
    down_weight_grads = jnp.zeros((N_TILE, TILE_W, D), jnp.bfloat16).at[tile_slot].set(down_tiles.reshape(TILES, TILE_W, D))
    layer_out = out_acc[:TOKENS].astype(jnp.bfloat16)
    token_grads = input_acc[:TOKENS].astype(jnp.bfloat16)
    gate_grads = gate_acc[:TOKENS * TOPK].reshape(TOKENS, TOPK)
    return layer_out, token_grads, gate_grads, gate_weight_grads, up_weight_grads, down_weight_grads
```

```python
import jax
import jax.numpy as jnp
import numpy as np
from jax import lax
from jax.experimental import pallas as pl
from jax.experimental.pallas import tpu as pltpu
from jax.sharding import Mesh
from jax.sharding import PartitionSpec as P

D = 2048
TOPK = 8
TILE_W = 128
HTILES = 6
CAP = 10
NY, NC, NX = 4, 2, 4
D_PART = D // NY
UNITS = TILE_W // (NX * NC)
HALF = HTILES // 2 * UNITS
SOURCES = NX * NC
GROUP = NY * CAP
LANES = SOURCES * GROUP
VMEM_LIMIT = 48 * 1024 * 1024

CONTRACT_COLS = (((1,), (1,)), ((), ()))
CONTRACT_ROWS = (((0,), (0,)), ((), ()))


def shifted(value, axis, size, step):
    return lax.ppermute(value, axis, [(i, (i + step) % size) for i in range(size)])


def exchanged(value):
    return shifted(value, "c", NC, 1)


def swap(value, axis):
    return lax.all_to_all(value, axis, split_axis=0, concat_axis=0, tiled=True)


def whole(shape):
    return pl.BlockSpec(shape, lambda e, *_: (0,) * len(shape))


def slice_kernel(place, gate_ref, up_ref, down_ref, out_ref, turned):
    core = place[1]
    for matrix, ref in enumerate((gate_ref, up_ref, down_ref)):
        turned[...] = ref[0] if matrix == 2 else ref[0].T
        for x in range(NX):
            start = pl.multiple_of(x * NC * UNITS + core * UNITS, UNITS)
            out_ref[x, matrix * UNITS : (matrix + 1) * UNITS, :] = turned[pl.ds(start, UNITS), :]


def weight_slices(place, w_gate, w_up, w_down):
    return pl.pallas_call(
        slice_kernel,
        grid_spec=pltpu.PrefetchScalarGridSpec(
            num_scalar_prefetch=1,
            grid=(1,),
            in_specs=[
                pl.BlockSpec((1, D_PART, TILE_W), lambda i, place: (0, place[0], 0)),
                pl.BlockSpec((1, D_PART, TILE_W), lambda i, place: (0, place[0], 0)),
                pl.BlockSpec((1, TILE_W, D_PART), lambda i, place: (0, 0, place[0])),
            ],
            out_specs=whole((NX, 3 * UNITS, D_PART)),
            scratch_shapes=[pltpu.VMEM((TILE_W, D_PART), jnp.bfloat16)],
        ),
        out_shape=jax.ShapeDtypeStruct((NX, 3 * UNITS, D_PART), jnp.bfloat16),
        compiler_params=pltpu.CompilerParams(vmem_limit_bytes=VMEM_LIMIT),
    )(place, w_gate, w_up, w_down)


def expert_weight(slots, weights_ref, expert, matrix, tiles):
    rows = slice(matrix * UNITS, (matrix + 1) * UNITS)
    return [weights_ref[slots[expert * HTILES + h], rows, :] for h in tiles]


def both_rows(row_refs):
    blocks = [ref[0].astype(jnp.float32) for ref in row_refs]
    inputs = jnp.concatenate([b[:GROUP] for b in blocks], axis=0)
    scaled = jnp.concatenate([b[GROUP:] for b in blocks], axis=0)
    return inputs.astype(jnp.bfloat16), scaled.astype(jnp.bfloat16)


def partial_kernel(slots, weights_ref, *refs):
    row_refs, out_ref = refs[:SOURCES], refs[SOURCES]
    expert = pl.program_id(0)
    inputs, scaled = both_rows(row_refs)
    for matrix, rows in ((0, inputs), (1, inputs), (2, scaled)):
        weight = jnp.concatenate(
            expert_weight(slots, weights_ref, expert, matrix, range(HTILES)), axis=0
        )
        product = lax.dot_general(
            weight, rows, CONTRACT_COLS, preferred_element_type=jnp.float32
        ).astype(jnp.bfloat16)
        out_ref[0, matrix] = product[:HALF]
        out_ref[1, matrix] = product[HALF:]


def row_specs():
    return [pl.BlockSpec((1, 2 * GROUP, D_PART), lambda e, *_: (e, 0, 0))] * SOURCES


def partial_products(slots, weights, rows, experts):
    return pl.pallas_call(
        partial_kernel,
        grid_spec=pltpu.PrefetchScalarGridSpec(
            num_scalar_prefetch=1,
            grid=(experts,),
            in_specs=[whole(weights.shape)] + row_specs(),
            out_specs=pl.BlockSpec((2, 3, HALF, LANES), lambda e, *_: (e, 0, 0, 0)),
        ),
        out_shape=jax.ShapeDtypeStruct((2 * experts, 3, HALF, LANES), jnp.bfloat16),
        compiler_params=pltpu.CompilerParams(vmem_limit_bytes=VMEM_LIMIT),
    )(slots, weights, *rows)


def activation(act_ref, matrix):
    return jnp.concatenate([act_ref[0, matrix], act_ref[1, matrix]], axis=0)


def weight_grad_kernel(slots, act_ref, *refs):
    row_refs, out_ref = refs[:SOURCES], refs[SOURCES]
    expert = pl.program_id(0)

    @pl.when(expert == 0)
    def _():
        out_ref[...] = jnp.zeros_like(out_ref)

    inputs, scaled = both_rows(row_refs)
    for matrix, rows in ((0, inputs), (1, inputs), (2, scaled)):
        grad = jnp.dot(
            activation(act_ref, matrix), rows, preferred_element_type=jnp.float32
        ).astype(jnp.bfloat16)
        for h in range(HTILES):
            out_ref[slots[expert * HTILES + h], matrix * UNITS : (matrix + 1) * UNITS, :] = grad[
                h * UNITS : (h + 1) * UNITS
            ]


def act_spec():
    return pl.BlockSpec((2, 3, HALF, LANES), lambda e, *_: (e, 0, 0, 0))


def weight_grads(slots, acts, rows, experts, tile_count):
    shape = (tile_count, 3 * UNITS, D_PART)
    return pl.pallas_call(
        weight_grad_kernel,
        grid_spec=pltpu.PrefetchScalarGridSpec(
            num_scalar_prefetch=1,
            grid=(experts,),
            in_specs=[act_spec()] + row_specs(),
            out_specs=whole(shape),
        ),
        out_shape=jax.ShapeDtypeStruct(shape, jnp.bfloat16),
        compiler_params=pltpu.CompilerParams(vmem_limit_bytes=VMEM_LIMIT),
    )(slots, acts, *rows)


def output_kernel(slots, weights_ref, act_ref, *out_refs):
    expert = pl.program_id(0)
    tiles = range(HTILES)
    out = lax.dot_general(
        activation(act_ref, 2),
        jnp.concatenate(expert_weight(slots, weights_ref, expert, 2, tiles), axis=0),
        CONTRACT_ROWS,
        preferred_element_type=jnp.float32,
    )
    back = lax.dot_general(
        jnp.concatenate([activation(act_ref, 0), activation(act_ref, 1)], axis=0),
        jnp.concatenate(
            expert_weight(slots, weights_ref, expert, 0, tiles)
            + expert_weight(slots, weights_ref, expert, 1, tiles),
            axis=0,
        ),
        CONTRACT_ROWS,
        preferred_element_type=jnp.float32,
    )
    for b, ref in enumerate(out_refs):
        part = slice(b * GROUP, (b + 1) * GROUP)
        ref[0] = jnp.concatenate([out[part], back[part]], axis=0).astype(jnp.bfloat16)


def outputs(slots, weights, acts, experts):
    return pl.pallas_call(
        output_kernel,
        grid_spec=pltpu.PrefetchScalarGridSpec(
            num_scalar_prefetch=1,
            grid=(experts,),
            in_specs=[whole(weights.shape), act_spec()],
            out_specs=row_specs(),
        ),
        out_shape=[jax.ShapeDtypeStruct((experts, 2 * GROUP, D_PART), jnp.bfloat16)] * SOURCES,
        compiler_params=pltpu.CompilerParams(vmem_limit_bytes=VMEM_LIMIT),
    )(slots, weights, acts)


def regroup_matrix(experts, sent):
    e, kind, y, r = np.meshgrid(
        np.arange(experts), np.arange(2), np.arange(NY), np.arange(CAP), indexing="ij"
    )
    source = y * sent + kind * experts * CAP + e * CAP + r
    matrix = np.zeros((source.size, NY * sent), np.float32)
    matrix[np.arange(source.size), source.reshape(-1)] = 1
    return jnp.asarray(matrix, jnp.bfloat16)


def per_device(tokens, expert_ids, gates, tile_slot, w_gate, w_up, w_down, grad_out):
    z_count = lax.axis_size("z")
    tok_rows = tokens.shape[0]
    experts = tile_slot.shape[0] // HTILES
    slot_count = experts * CAP
    sent = -(-2 * slot_count // 16) * 16
    core = lax.axis_index("c")
    place = jnp.stack([lax.axis_index("y"), core]).astype(jnp.int32)
    slots = (tile_slot % z_count) * NX + tile_slot // z_count

    weight_parts = swap(weight_slices(place, w_gate, w_up, w_down), "x")
    weights = lax.all_gather(weight_parts, "z", axis=0, tiled=True)

    route_ids = expert_ids.reshape(-1)
    member = (route_ids[:, None] == jnp.arange(experts, dtype=jnp.int32)[None, :]).astype(jnp.int32)
    slot_rank = jnp.sum((jnp.cumsum(member, axis=0) - member) * member, axis=1)
    position = jnp.where(route_ids < experts, route_ids * CAP + slot_rank, slot_count)
    choose = (position[:, None] == jnp.arange(slot_count, dtype=jnp.int32)[None, :]).astype(
        jnp.float32
    )
    picker = jnp.sum(choose.reshape(tok_rows, TOPK, slot_count), axis=1)
    picker_half = picker.astype(jnp.bfloat16)
    gate_slot = jnp.dot(gates.reshape(-1), choose, precision=lax.Precision.HIGHEST)

    expert_rows = lax.dot_general(
        picker_half, tokens, CONTRACT_ROWS, preferred_element_type=jnp.float32
    ).astype(jnp.bfloat16)
    upstream = lax.dot_general(
        picker_half, grad_out, CONTRACT_ROWS, preferred_element_type=jnp.float32
    )
    scaled = (gate_slot[:, None] * upstream).astype(jnp.bfloat16)
    both = jnp.concatenate([expert_rows, scaled], axis=0)
    both = jnp.pad(both, ((0, sent - 2 * slot_count), (0, 0)))
    both = both.reshape(sent, NY, D_PART).transpose(1, 0, 2)
    regroup = regroup_matrix(experts, sent)
    own_rows = (
        jnp.dot(
            regroup,
            swap(both, "y").reshape(NY * sent, D_PART),
            preferred_element_type=jnp.float32,
        )
        .astype(jnp.bfloat16)
        .reshape(experts, 2 * GROUP, D_PART)
    )
    steps = (1, 3, 2)
    rows = [own_rows] + [shifted(own_rows, "x", NX, step) for step in steps]
    rows = rows + [exchanged(block) for block in rows]

    partial = swap(partial_products(slots, weights, rows, experts), "y")
    pieces = partial.shape[0] // NY
    total = jnp.sum(partial.reshape(NY, pieces, 3, HALF, LANES).astype(jnp.float32), axis=0)
    pre_gate, pre_up, hidden_grad = total[:, 0], total[:, 1], total[:, 2]
    sigmoid_gate = jax.nn.sigmoid(pre_gate)
    activated = pre_gate * sigmoid_gate
    acts = jnp.stack(
        [
            hidden_grad * pre_up * sigmoid_gate * (1.0 + pre_gate * (1.0 - sigmoid_gate)),
            hidden_grad * activated,
            activated * pre_up,
        ],
        axis=1,
    ).astype(jnp.bfloat16)
    acts = swap(jnp.tile(acts, (NY, 1, 1, 1)), "y")

    grads = weight_grads(slots, acts, rows, experts, z_count * NX)
    grads = lax.psum_scatter(grads, "z", scatter_dimension=0, tiled=True)
    grads = swap(grads, "x")
    half = D_PART // NC
    keep = lax.dynamic_slice_in_dim(grads, core * half, half, axis=2)
    give = lax.dynamic_slice_in_dim(grads, (1 - core) * half, half, axis=2)
    take = exchanged(give)
    pair = jnp.stack([jnp.where(core == 0, keep, take), jnp.where(core == 0, take, keep)], axis=1)
    pair = pair.reshape(NX, NC, 3, UNITS, half).transpose(2, 0, 1, 3, 4).reshape(3, TILE_W, half)
    gate_weight_grads = pair[0].T[None]
    up_weight_grads = pair[1].T[None]
    down_weight_grads = pair[2][None]

    blocks = outputs(slots, weights, acts, experts)
    far = [exchanged(block) for block in blocks[NX:]]
    near = [
        (a.astype(jnp.float32) + b.astype(jnp.float32)).astype(jnp.bfloat16)
        for a, b in zip(blocks[:NX], far, strict=True)
    ]
    home = near[0].astype(jnp.float32)
    for block, step in zip(near[1:], steps, strict=True):
        home = home + shifted(block, "x", NX, NX - step).astype(jnp.float32)
    home = lax.dot_general(
        regroup,
        home.astype(jnp.bfloat16).reshape(experts * 2 * GROUP, D_PART),
        CONTRACT_ROWS,
        preferred_element_type=jnp.float32,
    ).astype(jnp.bfloat16)
    home = swap(home.reshape(NY, sent, D_PART), "y").transpose(1, 0, 2).reshape(sent, D)
    expert_out = home[:slot_count].astype(jnp.float32)
    input_slot = home[slot_count : 2 * slot_count].astype(jnp.float32)
    layer_out = jnp.dot(
        picker, gate_slot[:, None] * expert_out, precision=lax.Precision.HIGHEST
    ).astype(jnp.bfloat16)
    gate_terms = jnp.sum(expert_out * upstream, axis=1)
    gate_grads = jnp.dot(choose, gate_terms, precision=lax.Precision.HIGHEST).reshape(
        tok_rows, TOPK
    )
    token_grads = jnp.dot(picker, input_slot, precision=lax.Precision.HIGHEST).astype(jnp.bfloat16)
    return (
        layer_out,
        token_grads,
        gate_grads,
        gate_weight_grads,
        up_weight_grads,
        down_weight_grads,
    )


def solution(mesh):
    dp, tile = ("y", "c"), ("x", "z")
    planes = Mesh(mesh.devices.reshape(NY, NC, NX, -1), dp + tile)
    rows = P(dp + tile, None)
    in_specs = (
        rows,
        rows,
        rows,
        P(),
        P(tile, None, None),
        P(tile, None, None),
        P(tile, None, None),
        rows,
    )
    out_specs = (
        rows,
        rows,
        rows,
        P(tile, dp, None),
        P(tile, dp, None),
        P(tile, None, dp),
    )
    return jax.shard_map(
        per_device, mesh=planes, in_specs=in_specs, out_specs=out_specs, check_vma=False
    )
```

```python
import jax
import jax.numpy as jnp
import numpy as np
from jax import lax
from jax.experimental import pallas as pl
from jax.experimental.pallas import tpu as pltpu
from jax.sharding import Mesh
from jax.sharding import PartitionSpec as P

D = 2048
TOPK = 8
TILE_W = 128
HTILES = 6
CAP = 10
NY, NC, NX = 4, 2, 4
D_PART = D // NY
UNITS = TILE_W // (NX * NC)
HALF = HTILES // 2 * UNITS
SOURCES = NX * NC
GROUP = NY * CAP
LANES = SOURCES * GROUP
PACKED = HALF * LANES // 128
STEP = 2
VMEM_LIMIT = 48 * 1024 * 1024

CONTRACT_COLS = (((1,), (1,)), ((), ()))
CONTRACT_ROWS = (((0,), (0,)), ((), ()))


def shifted(value, axis, size, step):
    return lax.ppermute(value, axis, [(i, (i + step) % size) for i in range(size)])


def exchanged(value):
    return shifted(value, "c", NC, 1)


def swap(value, axis):
    return lax.all_to_all(value, axis, split_axis=0, concat_axis=0, tiled=True)


def whole(shape):
    return pl.BlockSpec(shape, lambda e, *_: (0,) * len(shape))


def slice_kernel(gate_ref, up_ref, down_ref, out_ref, gate, up, down, turned, sems):
    core = lax.axis_index("c")
    part = pl.ds(pl.multiple_of(lax.axis_index("y") * D_PART, D_PART), D_PART)
    copies = [
        pltpu.make_async_copy(gate_ref.at[0, part, :], gate, sems.at[0]),
        pltpu.make_async_copy(up_ref.at[0, part, :], up, sems.at[1]),
        pltpu.make_async_copy(down_ref.at[0, :, part], down, sems.at[2]),
    ]
    for copy in copies:
        copy.start()
    for matrix, (copy, part_ref) in enumerate(zip(copies, (gate, up, down), strict=True)):
        copy.wait()
        if matrix < 2:
            turned[...] = part_ref[...].T
            part_ref = turned
        for x in range(NX):
            start = pl.multiple_of(x * NC * UNITS + core * UNITS, UNITS)
            out_ref[x, matrix * UNITS : (matrix + 1) * UNITS, :] = part_ref[pl.ds(start, UNITS), :]


def weight_slices(w_gate, w_up, w_down):
    return pl.pallas_call(
        slice_kernel,
        in_specs=[pl.BlockSpec(memory_space=pltpu.HBM)] * 3,
        out_shape=jax.ShapeDtypeStruct((NX, 3 * UNITS, D_PART), jnp.bfloat16),
        scratch_shapes=[
            pltpu.VMEM((D_PART, TILE_W), jnp.bfloat16),
            pltpu.VMEM((D_PART, TILE_W), jnp.bfloat16),
            pltpu.VMEM((TILE_W, D_PART), jnp.bfloat16),
            pltpu.VMEM((TILE_W, D_PART), jnp.bfloat16),
            pltpu.SemaphoreType.DMA((3,)),
        ],
        compiler_params=pltpu.CompilerParams(vmem_limit_bytes=VMEM_LIMIT),
    )(w_gate, w_up, w_down)


def parted_kernel(*refs):
    row_refs, (inputs_ref, scaled_ref) = refs[:NX], refs[NX:]
    blocks = [ref[...].astype(jnp.float32) for ref in row_refs]
    inputs_ref[...] = jnp.concatenate([b[:, :GROUP] for b in blocks], axis=1).astype(jnp.bfloat16)
    scaled_ref[...] = jnp.concatenate([b[:, GROUP:] for b in blocks], axis=1).astype(jnp.bfloat16)


def parted_rows(blocks, experts):
    return pl.pallas_call(
        parted_kernel,
        grid=(experts // STEP,),
        in_specs=[expert_spec(2 * GROUP)] * NX,
        out_specs=[expert_spec(NX * GROUP)] * 2,
        out_shape=[jax.ShapeDtypeStruct((experts, NX * GROUP, D_PART), jnp.bfloat16)] * 2,
        compiler_params=pltpu.CompilerParams(vmem_limit_bytes=VMEM_LIMIT),
    )(*blocks)


def expert_spec(rows):
    return pl.BlockSpec((STEP, rows, D_PART), lambda e, *_: (e, 0, 0))


def piece_spec():
    return pl.BlockSpec((2 * STEP, 3 * PACKED, 128), lambda e, *_: (e, 0, 0))


def expert_weight(slots, weights_ref, expert, matrix):
    rows = slice(matrix * UNITS, (matrix + 1) * UNITS)
    return jnp.concatenate(
        [weights_ref[slots[expert * HTILES + h], rows, :] for h in range(HTILES)], axis=0
    )


def packed(values):
    mid = HALF // 2
    rest = jnp.concatenate([values[:mid, 256:], values[mid:, 256:]], axis=1)
    return jnp.concatenate([values[:, :128], values[:, 128:256], rest], axis=0)


def unpacked(values):
    rest = values[2 * HALF :]
    rest = jnp.concatenate([rest[:, :64], rest[:, 64:]], axis=0)
    return jnp.concatenate([values[:HALF], values[HALF : 2 * HALF], rest], axis=1)


def partial_kernel(slots, weights_ref, *refs):
    near_inputs, near_scaled, far_inputs, far_scaled, out_ref = refs
    for i in range(STEP):
        expert = pl.program_id(0) * STEP + i
        inputs = jnp.concatenate([near_inputs[i], far_inputs[i]], axis=0)
        scaled = jnp.concatenate([near_scaled[i], far_scaled[i]], axis=0)
        products = [
            lax.dot_general(
                expert_weight(slots, weights_ref, expert, matrix),
                rows,
                CONTRACT_COLS,
                preferred_element_type=jnp.float32,
            )
            for matrix, rows in ((0, inputs), (1, inputs), (2, scaled))
        ]
        for half in range(2):
            part = slice(half * HALF, (half + 1) * HALF)
            out_ref[2 * i + half] = jnp.concatenate(
                [packed(p[part]) for p in products], axis=0
            ).astype(jnp.bfloat16)


def partial_products(slots, weights, rows, experts):
    return pl.pallas_call(
        partial_kernel,
        grid_spec=pltpu.PrefetchScalarGridSpec(
            num_scalar_prefetch=1,
            grid=(experts // STEP,),
            in_specs=[whole(weights.shape)] + [expert_spec(NX * GROUP)] * 4,
            out_specs=piece_spec(),
        ),
        out_shape=jax.ShapeDtypeStruct((2 * experts, 3 * PACKED, 128), jnp.bfloat16),
        compiler_params=pltpu.CompilerParams(vmem_limit_bytes=VMEM_LIMIT),
    )(slots, weights, *rows)


def activations(act_ref, i):
    pieces = [act_ref[2 * i + half].astype(jnp.float32) for half in range(2)]
    return [
        jnp.concatenate(
            [unpacked(p[matrix * PACKED : (matrix + 1) * PACKED]) for p in pieces], axis=0
        ).astype(jnp.bfloat16)
        for matrix in range(3)
    ]


def weight_grad_kernel(slots, act_ref, *refs):
    near_inputs, near_scaled, far_inputs, far_scaled, out_ref = refs

    @pl.when(pl.program_id(0) == 0)
    def _():
        out_ref[...] = jnp.zeros_like(out_ref)

    for i in range(STEP):
        expert = pl.program_id(0) * STEP + i
        inputs = jnp.concatenate([near_inputs[i], far_inputs[i]], axis=0)
        scaled = jnp.concatenate([near_scaled[i], far_scaled[i]], axis=0)
        acts = activations(act_ref, i)
        for matrix, rows in enumerate((inputs, inputs, scaled)):
            grad = jnp.dot(acts[matrix], rows, preferred_element_type=jnp.float32)
            grad = grad.astype(jnp.bfloat16)
            for h in range(HTILES):
                slot = slots[expert * HTILES + h]
                out_ref[slot, matrix * UNITS : (matrix + 1) * UNITS, :] = grad[
                    h * UNITS : (h + 1) * UNITS
                ]


def weight_grads(slots, acts, rows, experts, tile_count):
    shape = (tile_count, 3 * UNITS, D_PART)
    return pl.pallas_call(
        weight_grad_kernel,
        grid_spec=pltpu.PrefetchScalarGridSpec(
            num_scalar_prefetch=1,
            grid=(experts // STEP,),
            in_specs=[piece_spec()] + [expert_spec(NX * GROUP)] * 4,
            out_specs=whole(shape),
        ),
        out_shape=jax.ShapeDtypeStruct(shape, jnp.bfloat16),
        compiler_params=pltpu.CompilerParams(vmem_limit_bytes=VMEM_LIMIT),
    )(slots, acts, *rows)


def output_kernel(slots, weights_ref, act_ref, *out_refs):
    for i in range(STEP):
        expert = pl.program_id(0) * STEP + i
        gate_pre_grad, up_pre_grad, hidden = activations(act_ref, i)
        gate, up, down = [expert_weight(slots, weights_ref, expert, m) for m in range(3)]
        out = lax.dot_general(hidden, down, CONTRACT_ROWS, preferred_element_type=jnp.float32)
        back = lax.dot_general(
            jnp.concatenate([gate_pre_grad, up_pre_grad], axis=0),
            jnp.concatenate([gate, up], axis=0),
            CONTRACT_ROWS,
            preferred_element_type=jnp.float32,
        )
        for b in range(SOURCES):
            part = slice(b * GROUP, (b + 1) * GROUP)
            block = jnp.concatenate([out[part], back[part]], axis=0).astype(jnp.bfloat16)
            if b < NX:
                out_refs[b][i] = block
            else:
                far = (b - NX) * 2 * GROUP
                out_refs[NX][i, far : far + 2 * GROUP] = block


def outputs(slots, weights, acts, experts):
    rows = [2 * GROUP] * NX + [NX * 2 * GROUP]
    return pl.pallas_call(
        output_kernel,
        grid_spec=pltpu.PrefetchScalarGridSpec(
            num_scalar_prefetch=1,
            grid=(experts // STEP,),
            in_specs=[whole(weights.shape), piece_spec()],
            out_specs=[expert_spec(r) for r in rows],
        ),
        out_shape=[jax.ShapeDtypeStruct((experts, r, D_PART), jnp.bfloat16) for r in rows],
        compiler_params=pltpu.CompilerParams(vmem_limit_bytes=VMEM_LIMIT),
    )(slots, weights, acts)


def regroup_matrix(experts, sent):
    e, kind, y, r = np.meshgrid(
        np.arange(experts), np.arange(2), np.arange(NY), np.arange(CAP), indexing="ij"
    )
    source = y * sent + kind * experts * CAP + e * CAP + r
    matrix = np.zeros((source.size, NY * sent), np.float32)
    matrix[np.arange(source.size), source.reshape(-1)] = 1
    return jnp.asarray(matrix, jnp.bfloat16)


def per_device(tokens, expert_ids, gates, tile_slot, w_gate, w_up, w_down, grad_out):
    z_count = lax.axis_size("z")
    tok_rows = tokens.shape[0]
    experts = tile_slot.shape[0] // HTILES
    slot_count = experts * CAP
    sent = -(-2 * slot_count // 16) * 16
    slots = (tile_slot % z_count) * NX + tile_slot // z_count

    weight_parts = swap(weight_slices(w_gate, w_up, w_down), "x")
    weights = lax.all_gather(weight_parts, "z", axis=0, tiled=True)

    route_ids = expert_ids.reshape(-1)
    member = (route_ids[:, None] == jnp.arange(experts, dtype=jnp.int32)[None, :]).astype(jnp.int32)
    slot_rank = jnp.sum((jnp.cumsum(member, axis=0) - member) * member, axis=1)
    position = jnp.where(route_ids < experts, route_ids * CAP + slot_rank, slot_count)
    choose = (position[:, None] == jnp.arange(slot_count, dtype=jnp.int32)[None, :]).astype(
        jnp.float32
    )
    picker = jnp.sum(choose.reshape(tok_rows, TOPK, slot_count), axis=1)
    picker_half = picker.astype(jnp.bfloat16)
    gate_slot = jnp.dot(gates.reshape(-1), choose, precision=lax.Precision.HIGHEST)

    expert_rows = lax.dot_general(
        picker_half, tokens, CONTRACT_ROWS, preferred_element_type=jnp.float32
    ).astype(jnp.bfloat16)
    upstream = lax.dot_general(
        picker_half, grad_out, CONTRACT_ROWS, preferred_element_type=jnp.float32
    )
    scaled = (gate_slot[:, None] * upstream).astype(jnp.bfloat16)
    both = jnp.concatenate([expert_rows, scaled], axis=0)
    both = jnp.pad(both, ((0, sent - 2 * slot_count), (0, 0)))
    both = both.reshape(sent, NY, D_PART).transpose(1, 0, 2)
    regroup = regroup_matrix(experts, sent)
    own_rows = (
        jnp.dot(
            regroup,
            swap(both, "y").reshape(NY * sent, D_PART),
            preferred_element_type=jnp.float32,
        )
        .astype(jnp.bfloat16)
        .reshape(experts, 2 * GROUP, D_PART)
    )
    steps = (1, 3, 2)
    blocks = [own_rows] + [shifted(own_rows, "x", NX, step) for step in steps]
    rows = list(parted_rows(blocks, experts))
    rows = rows + [exchanged(block) for block in rows]

    partial = swap(partial_products(slots, weights, rows, experts), "y")
    pieces = partial.shape[0] // NY
    total = jnp.sum(partial.reshape(NY, pieces, 3 * PACKED, 128).astype(jnp.float32), axis=0)
    pre_gate, pre_up, hidden_grad = [
        total[:, matrix * PACKED : (matrix + 1) * PACKED] for matrix in range(3)
    ]
    sigmoid_gate = jax.nn.sigmoid(pre_gate)
    activated = pre_gate * sigmoid_gate
    acts = jnp.concatenate(
        [
            hidden_grad * pre_up * sigmoid_gate * (1.0 + pre_gate * (1.0 - sigmoid_gate)),
            hidden_grad * activated,
            activated * pre_up,
        ],
        axis=1,
    ).astype(jnp.bfloat16)
    acts = swap(jnp.tile(acts, (NY, 1, 1)), "y")

    grads = weight_grads(slots, acts, rows, experts, z_count * NX)
    grads = lax.psum_scatter(grads, "z", scatter_dimension=0, tiled=True)
    half = D_PART // NC
    grads = grads.reshape(NX, 3 * UNITS, NC, half).transpose(0, 2, 1, 3)
    grads = swap(grads.reshape(NX * NC, 3 * UNITS, half), ("x", "c"))
    grads = grads.reshape(NX * NC, 3, UNITS, half).transpose(1, 0, 2, 3).reshape(3, TILE_W, half)
    gate_weight_grads = grads[0].T[None]
    up_weight_grads = grads[1].T[None]
    down_weight_grads = grads[2][None]

    blocks = outputs(slots, weights, acts, experts)
    far = exchanged(blocks[NX])
    near = [
        (
            block.astype(jnp.float32)
            + far[:, i * 2 * GROUP : (i + 1) * 2 * GROUP].astype(jnp.float32)
        ).astype(jnp.bfloat16)
        for i, block in enumerate(blocks[:NX])
    ]
    home = near[0].astype(jnp.float32)
    for block, step in zip(near[1:], steps, strict=True):
        home = home + shifted(block, "x", NX, NX - step).astype(jnp.float32)
    home = lax.dot_general(
        regroup,
        home.astype(jnp.bfloat16).reshape(experts * 2 * GROUP, D_PART),
        CONTRACT_ROWS,
        preferred_element_type=jnp.float32,
    ).astype(jnp.bfloat16)
    home = swap(home.reshape(NY, sent, D_PART), "y").transpose(1, 0, 2).reshape(sent, D)
    expert_out = home[:slot_count].astype(jnp.float32)
    input_slot = home[slot_count : 2 * slot_count].astype(jnp.float32)
    layer_out = jnp.dot(
        picker, gate_slot[:, None] * expert_out, precision=lax.Precision.HIGHEST
    ).astype(jnp.bfloat16)
    gate_terms = jnp.sum(expert_out * upstream, axis=1)
    gate_grads = jnp.dot(choose, gate_terms, precision=lax.Precision.HIGHEST).reshape(
        tok_rows, TOPK
    )
    token_grads = jnp.dot(picker, input_slot, precision=lax.Precision.HIGHEST).astype(jnp.bfloat16)
    return (
        layer_out,
        token_grads,
        gate_grads,
        gate_weight_grads,
        up_weight_grads,
        down_weight_grads,
    )


def solution(mesh):
    dp, tile = ("y", "c"), ("x", "z")
    planes = Mesh(mesh.devices.reshape(NY, NC, NX, -1), dp + tile)
    rows = P(dp + tile, None)
    in_specs = (
        rows,
        rows,
        rows,
        P(),
        P(tile, None, None),
        P(tile, None, None),
        P(tile, None, None),
        rows,
    )
    out_specs = (
        rows,
        rows,
        rows,
        P(tile, dp, None),
        P(tile, dp, None),
        P(tile, None, dp),
    )
    return jax.shard_map(
        per_device, mesh=planes, in_specs=in_specs, out_specs=out_specs, check_vma=False
    )
```

```python
import functools

import jax
import jax.numpy as jnp
import numpy as np
from jax import lax
from jax.experimental import pallas as pl
from jax.experimental.pallas import tpu as pltpu
from jax.sharding import Mesh
from jax.sharding import PartitionSpec as P

D = 2048
TOPK = 8
TILE_W = 128
HTILES = 6
CAP = 10
NY, NC, NX = 4, 2, 4
D_PART = D // NY
UNITS = TILE_W // (NX * NC)
HALF = HTILES // 2 * UNITS
SOURCES = NX * NC
GROUP = NY * CAP
LANES = SOURCES * GROUP
PACKED = HALF * LANES // 128
STEP = 2
VMEM_LIMIT = 20 * 1024 * 1024
WIDE_VMEM_LIMIT = 60 * 1024 * 1024
PARTS = ((0, 6), (6, 4))
STEPS = (1, 3, 2)

CONTRACT_COLS = (((1,), (1,)), ((), ()))
CONTRACT_ROWS = (((0,), (0,)), ((), ()))


def shifted(value, axis, size, step):
    return lax.ppermute(value, axis, [(i, (i + step) % size) for i in range(size)])


def exchanged(value):
    return shifted(value, "c", NC, 1)


def swap(value, axis):
    return lax.all_to_all(value, axis, split_axis=0, concat_axis=0, tiled=True)


def whole(shape):
    return pl.BlockSpec(shape, lambda e, *_: (0,) * len(shape))


def slice_kernel(gate_ref, up_ref, down_ref, out_ref, gate, up, down, turned, sems):
    core = lax.axis_index("c")
    part = pl.ds(pl.multiple_of(lax.axis_index("y") * D_PART, D_PART), D_PART)
    copies = [
        pltpu.make_async_copy(gate_ref.at[0, part, :], gate, sems.at[0]),
        pltpu.make_async_copy(up_ref.at[0, part, :], up, sems.at[1]),
        pltpu.make_async_copy(down_ref.at[0, :, part], down, sems.at[2]),
    ]
    for copy in copies:
        copy.start()
    for matrix, (copy, part_ref) in enumerate(zip(copies, (gate, up, down), strict=True)):
        copy.wait()
        if matrix < 2:
            turned[...] = part_ref[...].T
            part_ref = turned
        for x in range(NX):
            start = pl.multiple_of(x * NC * UNITS + core * UNITS, UNITS)
            out_ref[x, matrix * UNITS : (matrix + 1) * UNITS, :] = part_ref[pl.ds(start, UNITS), :]


def weight_slices(w_gate, w_up, w_down):
    return pl.pallas_call(
        slice_kernel,
        in_specs=[pl.BlockSpec(memory_space=pl.ANY)] * 3,
        out_shape=jax.ShapeDtypeStruct((NX, 3 * UNITS, D_PART), jnp.bfloat16),
        scratch_shapes=[
            pltpu.VMEM((D_PART, TILE_W), jnp.bfloat16),
            pltpu.VMEM((D_PART, TILE_W), jnp.bfloat16),
            pltpu.VMEM((TILE_W, D_PART), jnp.bfloat16),
            pltpu.VMEM((TILE_W, D_PART), jnp.bfloat16),
            pltpu.SemaphoreType.DMA((3,)),
        ],
        compiler_params=pltpu.CompilerParams(vmem_limit_bytes=WIDE_VMEM_LIMIT),
    )(w_gate, w_up, w_down)


def parted_kernel(*refs):
    row_refs, (inputs_ref, scaled_ref) = refs[:NX], refs[NX:]
    blocks = [ref[...].astype(jnp.float32) for ref in row_refs]
    inputs_ref[...] = jnp.concatenate([b[:, :GROUP] for b in blocks], axis=1).astype(jnp.bfloat16)
    scaled_ref[...] = jnp.concatenate([b[:, GROUP:] for b in blocks], axis=1).astype(jnp.bfloat16)


def parted_rows(blocks, experts):
    return pl.pallas_call(
        parted_kernel,
        grid=(experts // STEP,),
        in_specs=[expert_spec(2 * GROUP)] * NX,
        out_specs=[expert_spec(NX * GROUP)] * 2,
        out_shape=[jax.ShapeDtypeStruct((experts, NX * GROUP, D_PART), jnp.bfloat16)] * 2,
        compiler_params=pltpu.CompilerParams(vmem_limit_bytes=VMEM_LIMIT),
    )(*blocks)


def expert_spec(rows):
    return pl.BlockSpec((STEP, rows, D_PART), lambda e, *_: (e, 0, 0))


def piece_spec(first=0):
    return pl.BlockSpec((2 * STEP, 3 * PACKED, 128), lambda e, *_: (e + first // STEP, 0, 0))


def expert_weight(slots, weights_ref, expert, matrix):
    rows = slice(matrix * UNITS, (matrix + 1) * UNITS)
    return jnp.concatenate(
        [weights_ref[slots[expert * HTILES + h], rows, :] for h in range(HTILES)], axis=0
    )


def packed(values):
    mid = HALF // 2
    rest = jnp.concatenate([values[:mid, 256:], values[mid:, 256:]], axis=1)
    return jnp.concatenate([values[:, :128], values[:, 128:256], rest], axis=0)


def unpacked(values):
    rest = values[2 * HALF :]
    rest = jnp.concatenate([rest[:, :64], rest[:, 64:]], axis=0)
    return jnp.concatenate([values[:HALF], values[HALF : 2 * HALF], rest], axis=1)


def partial_kernel(experts, slots, weights, near_inputs, near_scaled, far_inputs, far_scaled, out):
    for expert in range(experts):
        gate, up, down = [expert_weight(slots, weights, expert, m) for m in range(3)]
        both = lax.dot_general(
            jnp.concatenate([gate, up], axis=0),
            jnp.concatenate([near_inputs[expert], far_inputs[expert]], axis=0),
            CONTRACT_COLS,
            preferred_element_type=jnp.float32,
        )
        grad = lax.dot_general(
            down,
            jnp.concatenate([near_scaled[expert], far_scaled[expert]], axis=0),
            CONTRACT_COLS,
            preferred_element_type=jnp.float32,
        )
        products = both[: 2 * HALF], both[2 * HALF :], grad
        for half in range(2):
            part = slice(half * HALF, (half + 1) * HALF)
            out[2 * expert + half] = jnp.concatenate(
                [packed(p[part]) for p in products], axis=0
            ).astype(jnp.bfloat16)


def in_vmem(count):
    smem = pl.BlockSpec(memory_space=pltpu.SMEM)
    return [smem] + [pl.BlockSpec(memory_space=pltpu.VMEM)] * count


def partial_products(slots, weights, rows, experts):
    return pl.pallas_call(
        functools.partial(partial_kernel, experts),
        in_specs=in_vmem(5),
        out_specs=pl.BlockSpec(memory_space=pltpu.VMEM),
        out_shape=jax.ShapeDtypeStruct((2 * experts, 3 * PACKED, 128), jnp.bfloat16),
        compiler_params=pltpu.CompilerParams(vmem_limit_bytes=VMEM_LIMIT),
    )(slots, weights, *rows)


def activations(act_ref, i):
    pieces = [act_ref[2 * i + half].astype(jnp.float32) for half in range(2)]
    return [
        jnp.concatenate(
            [unpacked(p[matrix * PACKED : (matrix + 1) * PACKED]) for p in pieces], axis=0
        ).astype(jnp.bfloat16)
        for matrix in range(3)
    ]


def weight_grad_kernel(
    experts, slots, acts, near_inputs, near_scaled, far_inputs, far_scaled, out
):
    out[...] = jnp.zeros_like(out)
    half = D_PART // NC
    for expert in range(experts):
        gate_pre_grad, up_pre_grad, hidden = activations(acts, expert)
        both = jnp.dot(
            jnp.concatenate([gate_pre_grad, up_pre_grad], axis=0),
            jnp.concatenate([near_inputs[expert], far_inputs[expert]], axis=0),
            preferred_element_type=jnp.float32,
        ).astype(jnp.bfloat16)
        down = jnp.dot(
            hidden,
            jnp.concatenate([near_scaled[expert], far_scaled[expert]], axis=0),
            preferred_element_type=jnp.float32,
        ).astype(jnp.bfloat16)
        for matrix, part in enumerate((both[: 2 * HALF], both[2 * HALF :], down)):
            rows = slice(matrix * UNITS, (matrix + 1) * UNITS)
            for h in range(HTILES):
                units = part[h * UNITS : (h + 1) * UNITS]
                slot = slots[expert * HTILES + h]
                for c in range(NC):
                    out[slot * NC + c, rows, :] = units[:, c * half : (c + 1) * half]


def weight_grads(slots, acts, rows, experts, tile_count):
    return pl.pallas_call(
        functools.partial(weight_grad_kernel, experts),
        in_specs=in_vmem(5),
        out_specs=pl.BlockSpec(memory_space=pltpu.VMEM),
        out_shape=jax.ShapeDtypeStruct(
            (tile_count * NC, 3 * UNITS, D_PART // NC), jnp.bfloat16
        ),
        compiler_params=pltpu.CompilerParams(vmem_limit_bytes=VMEM_LIMIT),
    )(slots, acts, *rows)


def output_kernel(first, slots, weights_ref, act_ref, *out_refs):
    for i in range(STEP):
        expert = first + pl.program_id(0) * STEP + i
        gate_pre_grad, up_pre_grad, hidden = activations(act_ref, i)
        gate, up, down = [expert_weight(slots, weights_ref, expert, m) for m in range(3)]
        out = lax.dot_general(hidden, down, CONTRACT_ROWS, preferred_element_type=jnp.float32)
        back = lax.dot_general(
            jnp.concatenate([gate_pre_grad, up_pre_grad], axis=0),
            jnp.concatenate([gate, up], axis=0),
            CONTRACT_ROWS,
            preferred_element_type=jnp.float32,
        )
        for b in range(SOURCES):
            part = slice(b * GROUP, (b + 1) * GROUP)
            block = jnp.concatenate([out[part], back[part]], axis=0).astype(jnp.bfloat16)
            if b < NX:
                out_refs[b][i] = block
            else:
                far = (b - NX) * 2 * GROUP
                out_refs[NX][i, far : far + 2 * GROUP] = block


def outputs(slots, weights, acts, first, experts):
    rows = [2 * GROUP] * NX + [NX * 2 * GROUP]
    return pl.pallas_call(
        functools.partial(output_kernel, first),
        grid_spec=pltpu.PrefetchScalarGridSpec(
            num_scalar_prefetch=1,
            grid=(experts // STEP,),
            in_specs=[whole(weights.shape), piece_spec(first)],
            out_specs=[expert_spec(r) for r in rows],
        ),
        out_shape=[jax.ShapeDtypeStruct((experts, r, D_PART), jnp.bfloat16) for r in rows],
        compiler_params=pltpu.CompilerParams(vmem_limit_bytes=VMEM_LIMIT),
    )(slots, weights, acts)


def regroup_matrix(experts, sent):
    e, kind, y, r = np.meshgrid(
        np.arange(experts), np.arange(2), np.arange(NY), np.arange(CAP), indexing="ij"
    )
    source = y * sent + kind * experts * CAP + e * CAP + r
    matrix = np.zeros((source.size, NY * sent), np.float32)
    matrix[np.arange(source.size), source.reshape(-1)] = 1
    return jnp.asarray(matrix, jnp.bfloat16)


def tile_grad_kernel(parts, gate, up, down):
    for matrix, ref in enumerate((gate, up, down)):
        rows = slice(matrix * UNITS, (matrix + 1) * UNITS)
        whole_tile = jnp.concatenate([parts[i, rows, :] for i in range(SOURCES)], axis=0)
        ref[0] = whole_tile if matrix == 2 else whole_tile.T


def tile_grads(parts):
    half = parts.shape[2]
    turned = jax.ShapeDtypeStruct((1, half, TILE_W), jnp.bfloat16)
    return pl.pallas_call(
        tile_grad_kernel,
        out_shape=[turned, turned, jax.ShapeDtypeStruct((1, TILE_W, half), jnp.bfloat16)],
        compiler_params=pltpu.CompilerParams(vmem_limit_bytes=VMEM_LIMIT),
    )(parts)


def sent_rows(experts):
    return -(-2 * experts * CAP // 16) * 16


def send_home(blocks, experts):
    sent = sent_rows(experts)
    far = exchanged(blocks[NX])
    near = [
        (
            block.astype(jnp.float32)
            + far[:, i * 2 * GROUP : (i + 1) * 2 * GROUP].astype(jnp.float32)
        ).astype(jnp.bfloat16)
        for i, block in enumerate(blocks[:NX])
    ]
    home = near[0].astype(jnp.float32)
    for block, step in zip(near[1:], STEPS, strict=True):
        home = home + shifted(block, "x", NX, NX - step).astype(jnp.float32)
    home = lax.dot_general(
        regroup_matrix(experts, sent),
        home.astype(jnp.bfloat16).reshape(experts * 2 * GROUP, D_PART),
        CONTRACT_ROWS,
        preferred_element_type=jnp.float32,
    ).astype(jnp.bfloat16)
    return swap(home.reshape(NY, sent, D_PART), "y").transpose(1, 0, 2).reshape(sent, D)


def per_device(tokens, expert_ids, gates, tile_slot, w_gate, w_up, w_down, grad_out):
    z_count = lax.axis_size("z")
    tok_rows = tokens.shape[0]
    experts = tile_slot.shape[0] // HTILES
    slot_count = experts * CAP
    sent = sent_rows(experts)
    slots = (tile_slot % z_count) * NX + tile_slot // z_count

    weight_parts = swap(weight_slices(w_gate, w_up, w_down), "x")
    weights = lax.all_gather(weight_parts, "z", axis=0, tiled=True)

    route_ids = expert_ids.reshape(-1)
    member = (route_ids[:, None] == jnp.arange(experts, dtype=jnp.int32)[None, :]).astype(jnp.int32)
    slot_rank = jnp.sum((jnp.cumsum(member, axis=0) - member) * member, axis=1)
    position = jnp.where(route_ids < experts, route_ids * CAP + slot_rank, slot_count)
    choose = (position[:, None] == jnp.arange(slot_count, dtype=jnp.int32)[None, :]).astype(
        jnp.float32
    )
    picker = jnp.sum(choose.reshape(tok_rows, TOPK, slot_count), axis=1)
    picker_half = picker.astype(jnp.bfloat16)
    gate_slot = jnp.dot(gates.reshape(-1), choose, precision=lax.Precision.HIGHEST)

    expert_rows = lax.dot_general(
        picker_half, tokens, CONTRACT_ROWS, preferred_element_type=jnp.float32
    ).astype(jnp.bfloat16)
    upstream = lax.dot_general(
        picker_half, grad_out, CONTRACT_ROWS, preferred_element_type=jnp.float32
    )
    scaled = (gate_slot[:, None] * upstream).astype(jnp.bfloat16)
    both = jnp.concatenate([expert_rows, scaled], axis=0)
    both = jnp.pad(both, ((0, sent - 2 * slot_count), (0, 0)))
    both = both.reshape(sent, NY, D_PART).transpose(1, 0, 2)
    regroup = regroup_matrix(experts, sent)
    own_rows = (
        jnp.dot(
            regroup,
            swap(both, "y").reshape(NY * sent, D_PART),
            preferred_element_type=jnp.float32,
        )
        .astype(jnp.bfloat16)
        .reshape(experts, 2 * GROUP, D_PART)
    )
    blocks = [own_rows] + [shifted(own_rows, "x", NX, step) for step in STEPS]
    rows = list(parted_rows(blocks, experts))
    rows = rows + [exchanged(block) for block in rows]

    partial = swap(partial_products(slots, weights, rows, experts), "y")
    pieces = partial.shape[0] // NY
    total = jnp.sum(partial.reshape(NY, pieces, 3 * PACKED, 128).astype(jnp.float32), axis=0)
    pre_gate, pre_up, hidden_grad = [
        total[:, matrix * PACKED : (matrix + 1) * PACKED] for matrix in range(3)
    ]
    sigmoid_gate = jax.nn.sigmoid(pre_gate)
    activated = pre_gate * sigmoid_gate
    acts = jnp.concatenate(
        [
            hidden_grad * pre_up * sigmoid_gate * (1.0 + pre_gate * (1.0 - sigmoid_gate)),
            hidden_grad * activated,
            activated * pre_up,
        ],
        axis=1,
    ).astype(jnp.bfloat16)
    acts = swap(jnp.tile(acts, (NY, 1, 1)), "y")

    grads = weight_grads(slots, acts, rows, experts, z_count * NX)
    grads, acts = lax.optimization_barrier((grads, acts))
    grads = swap(lax.psum_scatter(grads, "z", scatter_dimension=0, tiled=True), ("x", "c"))
    gate_weight_grads, up_weight_grads, down_weight_grads = tile_grads(grads)

    layer_out, gate_grads, token_grads = 0.0, 0.0, 0.0
    for first, count in PARTS:
        home = send_home(outputs(slots, weights, acts, first, count), count)
        here = slice(first * CAP, (first + count) * CAP)
        expert_out = home[: count * CAP].astype(jnp.float32)
        input_slot = home[count * CAP : 2 * count * CAP].astype(jnp.float32)
        layer_out += jnp.dot(
            picker[:, here], gate_slot[here, None] * expert_out, precision=lax.Precision.HIGHEST
        )
        gate_terms = jnp.sum(expert_out * upstream[here], axis=1)
        gate_grads += jnp.dot(choose[:, here], gate_terms, precision=lax.Precision.HIGHEST)
        token_grads += jnp.dot(picker[:, here], input_slot, precision=lax.Precision.HIGHEST)
    layer_out = layer_out.astype(jnp.bfloat16)
    token_grads = token_grads.astype(jnp.bfloat16)
    gate_grads = gate_grads.reshape(tok_rows, TOPK)
    return (
        layer_out,
        token_grads,
        gate_grads,
        gate_weight_grads,
        up_weight_grads,
        down_weight_grads,
    )


def solution(mesh):
    dp, tile = ("y", "c"), ("x", "z")
    planes = Mesh(mesh.devices.reshape(NY, NC, NX, -1), dp + tile)
    rows = P(dp + tile, None)
    in_specs = (
        rows,
        rows,
        rows,
        P(),
        P(tile, None, None),
        P(tile, None, None),
        P(tile, None, None),
        rows,
    )
    out_specs = (
        rows,
        rows,
        rows,
        P(tile, dp, None),
        P(tile, dp, None),
        P(tile, None, dp),
    )
    return jax.shard_map(
        per_device, mesh=planes, in_specs=in_specs, out_specs=out_specs, check_vma=False
    )
```

```python
import functools

import jax
import jax.numpy as jnp
import numpy as np
from jax import lax
from jax.experimental import pallas as pl
from jax.experimental.pallas import tpu as pltpu
from jax.sharding import Mesh
from jax.sharding import PartitionSpec as P

D = 2048
TOPK = 8
TILE_W = 128
HTILES = 6
CAP = 10
NY, NC, NX = 4, 2, 4
D_PART = D // NY
UNITS = TILE_W // (NX * NC)
HALF = HTILES // 2 * UNITS
SOURCES = NX * NC
GROUP = NY * CAP
LANES = SOURCES * GROUP
PACKED = HALF * LANES // 128
STEP = 2
VMEM_LIMIT = 20 * 1024 * 1024
WIDE_VMEM_LIMIT = 60 * 1024 * 1024
PARTS = ((0, 6), (6, 4))
STEPS = (1, 3, 2)

CONTRACT_COLS = (((1,), (1,)), ((), ()))
CONTRACT_ROWS = (((0,), (0,)), ((), ()))


def shifted(value, axis, size, step):
    return lax.ppermute(value, axis, [(i, (i + step) % size) for i in range(size)])


def exchanged(value):
    return shifted(value, "c", NC, 1)


def swap(value, axis):
    return lax.all_to_all(value, axis, split_axis=0, concat_axis=0, tiled=True)


def whole(shape):
    return pl.BlockSpec(shape, lambda e, *_: (0,) * len(shape))


def slice_kernel(gate_ref, up_ref, down_ref, out_ref, gate, up, down, turned, sems):
    core = lax.axis_index("c")
    part = pl.ds(pl.multiple_of(lax.axis_index("y") * D_PART, D_PART), D_PART)
    copies = [
        pltpu.make_async_copy(gate_ref.at[0, part, :], gate, sems.at[0]),
        pltpu.make_async_copy(up_ref.at[0, part, :], up, sems.at[1]),
        pltpu.make_async_copy(down_ref.at[0, :, part], down, sems.at[2]),
    ]
    for copy in copies:
        copy.start()
    for matrix, (copy, part_ref) in enumerate(zip(copies, (gate, up, down), strict=True)):
        copy.wait()
        if matrix < 2:
            turned[...] = part_ref[...].T
            part_ref = turned
        for x in range(NX):
            start = pl.multiple_of(x * NC * UNITS + core * UNITS, UNITS)
            out_ref[x, matrix * UNITS : (matrix + 1) * UNITS, :] = part_ref[pl.ds(start, UNITS), :]


def weight_slices(w_gate, w_up, w_down):
    return pl.pallas_call(
        slice_kernel,
        in_specs=[pl.BlockSpec(memory_space=pl.ANY)] * 3,
        out_shape=jax.ShapeDtypeStruct((NX, 3 * UNITS, D_PART), jnp.bfloat16),
        scratch_shapes=[
            pltpu.VMEM((D_PART, TILE_W), jnp.bfloat16),
            pltpu.VMEM((D_PART, TILE_W), jnp.bfloat16),
            pltpu.VMEM((TILE_W, D_PART), jnp.bfloat16),
            pltpu.VMEM((TILE_W, D_PART), jnp.bfloat16),
            pltpu.SemaphoreType.DMA((3,)),
        ],
        compiler_params=pltpu.CompilerParams(vmem_limit_bytes=WIDE_VMEM_LIMIT),
    )(w_gate, w_up, w_down)


def parted_kernel(*refs):
    row_refs, (inputs_ref, scaled_ref) = refs[:NX], refs[NX:]
    blocks = [ref[...].astype(jnp.float32) for ref in row_refs]
    inputs_ref[...] = jnp.concatenate([b[:, :GROUP] for b in blocks], axis=1).astype(jnp.bfloat16)
    scaled_ref[...] = jnp.concatenate([b[:, GROUP:] for b in blocks], axis=1).astype(jnp.bfloat16)


def parted_rows(blocks, experts):
    return pl.pallas_call(
        parted_kernel,
        grid=(experts // STEP,),
        in_specs=[expert_spec(2 * GROUP)] * NX,
        out_specs=[expert_spec(NX * GROUP)] * 2,
        out_shape=[jax.ShapeDtypeStruct((experts, NX * GROUP, D_PART), jnp.bfloat16)] * 2,
        compiler_params=pltpu.CompilerParams(vmem_limit_bytes=VMEM_LIMIT),
    )(*blocks)


def expert_spec(rows):
    return pl.BlockSpec((STEP, rows, D_PART), lambda e, *_: (e, 0, 0))


def piece_spec(first=0):
    return pl.BlockSpec((2 * STEP, 3 * PACKED, 128), lambda e, *_: (e + first // STEP, 0, 0))


def expert_weight(slots, weights_ref, expert, matrix):
    rows = slice(matrix * UNITS, (matrix + 1) * UNITS)
    return jnp.concatenate(
        [weights_ref[slots[expert * HTILES + h], rows, :] for h in range(HTILES)], axis=0
    )


def packed(values):
    mid = HALF // 2
    rest = jnp.concatenate([values[:mid, 256:], values[mid:, 256:]], axis=1)
    return jnp.concatenate([values[:, :128], values[:, 128:256], rest], axis=0)


def unpacked(values):
    rest = values[2 * HALF :]
    rest = jnp.concatenate([rest[:, :64], rest[:, 64:]], axis=0)
    return jnp.concatenate([values[:HALF], values[HALF : 2 * HALF], rest], axis=1)


def partial_kernel(experts, slots, weights, near_inputs, near_scaled, far_inputs, far_scaled, out):
    for expert in range(experts):
        gate, up, down = [expert_weight(slots, weights, expert, m) for m in range(3)]
        both = lax.dot_general(
            jnp.concatenate([gate, up], axis=0),
            jnp.concatenate([near_inputs[expert], far_inputs[expert]], axis=0),
            CONTRACT_COLS,
            preferred_element_type=jnp.float32,
        )
        grad = lax.dot_general(
            down,
            jnp.concatenate([near_scaled[expert], far_scaled[expert]], axis=0),
            CONTRACT_COLS,
            preferred_element_type=jnp.float32,
        )
        products = both[: 2 * HALF], both[2 * HALF :], grad
        for half in range(2):
            part = slice(half * HALF, (half + 1) * HALF)
            out[2 * expert + half] = jnp.concatenate(
                [packed(p[part]) for p in products], axis=0
            ).astype(jnp.bfloat16)


def in_vmem(count):
    smem = pl.BlockSpec(memory_space=pltpu.SMEM)
    return [smem] + [pl.BlockSpec(memory_space=pltpu.VMEM)] * count


def partial_products(slots, weights, rows, experts):
    return pl.pallas_call(
        functools.partial(partial_kernel, experts),
        in_specs=in_vmem(5),
        out_specs=pl.BlockSpec(memory_space=pltpu.VMEM),
        out_shape=jax.ShapeDtypeStruct((2 * experts, 3 * PACKED, 128), jnp.bfloat16),
        compiler_params=pltpu.CompilerParams(vmem_limit_bytes=VMEM_LIMIT),
    )(slots, weights, *rows)


def activations(act_ref, i):
    pieces = [act_ref[2 * i + half].astype(jnp.float32) for half in range(2)]
    return [
        jnp.concatenate(
            [unpacked(p[matrix * PACKED : (matrix + 1) * PACKED]) for p in pieces], axis=0
        ).astype(jnp.bfloat16)
        for matrix in range(3)
    ]


def weight_grad_kernel(
    experts, slots, acts, near_inputs, near_scaled, far_inputs, far_scaled, out
):
    out[...] = jnp.zeros_like(out)
    half = D_PART // NC
    for expert in range(experts):
        gate_pre_grad, up_pre_grad, hidden = activations(acts, expert)
        both = jnp.dot(
            jnp.concatenate([gate_pre_grad, up_pre_grad], axis=0),
            jnp.concatenate([near_inputs[expert], far_inputs[expert]], axis=0),
            preferred_element_type=jnp.float32,
        ).astype(jnp.bfloat16)
        down = jnp.dot(
            hidden,
            jnp.concatenate([near_scaled[expert], far_scaled[expert]], axis=0),
            preferred_element_type=jnp.float32,
        ).astype(jnp.bfloat16)
        for matrix, part in enumerate((both[: 2 * HALF], both[2 * HALF :], down)):
            rows = slice(matrix * UNITS, (matrix + 1) * UNITS)
            for h in range(HTILES):
                units = part[h * UNITS : (h + 1) * UNITS]
                slot = slots[expert * HTILES + h]
                for c in range(NC):
                    out[slot * NC + c, rows, :] = units[:, c * half : (c + 1) * half]


def weight_grads(slots, acts, rows, experts, tile_count):
    return pl.pallas_call(
        functools.partial(weight_grad_kernel, experts),
        in_specs=in_vmem(5),
        out_specs=pl.BlockSpec(memory_space=pltpu.VMEM),
        out_shape=jax.ShapeDtypeStruct(
            (tile_count * NC, 3 * UNITS, D_PART // NC), jnp.bfloat16
        ),
        compiler_params=pltpu.CompilerParams(vmem_limit_bytes=VMEM_LIMIT),
    )(slots, acts, *rows)


def output_kernel(first, slots, weights_ref, act_ref, *out_refs):
    for i in range(STEP):
        expert = first + pl.program_id(0) * STEP + i
        gate_pre_grad, up_pre_grad, hidden = activations(act_ref, i)
        gate, up, down = [expert_weight(slots, weights_ref, expert, m) for m in range(3)]
        out = lax.dot_general(hidden, down, CONTRACT_ROWS, preferred_element_type=jnp.float32)
        back = lax.dot_general(
            jnp.concatenate([gate_pre_grad, up_pre_grad], axis=0),
            jnp.concatenate([gate, up], axis=0),
            CONTRACT_ROWS,
            preferred_element_type=jnp.float32,
        )
        for b in range(SOURCES):
            part = slice(b * GROUP, (b + 1) * GROUP)
            block = jnp.concatenate([out[part], back[part]], axis=0).astype(jnp.bfloat16)
            if b < NX:
                out_refs[b][i] = block
            else:
                far = (b - NX) * 2 * GROUP
                out_refs[NX][i, far : far + 2 * GROUP] = block


def outputs(slots, weights, acts, first, experts):
    rows = [2 * GROUP] * NX + [NX * 2 * GROUP]
    return pl.pallas_call(
        functools.partial(output_kernel, first),
        grid_spec=pltpu.PrefetchScalarGridSpec(
            num_scalar_prefetch=1,
            grid=(experts // STEP,),
            in_specs=[whole(weights.shape), piece_spec(first)],
            out_specs=[expert_spec(r) for r in rows],
        ),
        out_shape=[jax.ShapeDtypeStruct((experts, r, D_PART), jnp.bfloat16) for r in rows],
        compiler_params=pltpu.CompilerParams(vmem_limit_bytes=VMEM_LIMIT),
    )(slots, weights, acts)


def regroup_matrix(experts, sent):
    e, kind, y, r = np.meshgrid(
        np.arange(experts), np.arange(2), np.arange(NY), np.arange(CAP), indexing="ij"
    )
    source = y * sent + kind * experts * CAP + e * CAP + r
    matrix = np.zeros((source.size, NY * sent), np.float32)
    matrix[np.arange(source.size), source.reshape(-1)] = 1
    return jnp.asarray(matrix, jnp.bfloat16)


def tile_grad_kernel(parts, gate, up, down):
    for matrix, ref in enumerate((gate, up, down)):
        rows = slice(matrix * UNITS, (matrix + 1) * UNITS)
        whole_tile = jnp.concatenate([parts[i, rows, :] for i in range(SOURCES)], axis=0)
        ref[0] = whole_tile if matrix == 2 else whole_tile.T


def tile_grads(parts):
    half = parts.shape[2]
    turned = jax.ShapeDtypeStruct((1, half, TILE_W), jnp.bfloat16)
    return pl.pallas_call(
        tile_grad_kernel,
        out_shape=[turned, turned, jax.ShapeDtypeStruct((1, TILE_W, half), jnp.bfloat16)],
        compiler_params=pltpu.CompilerParams(vmem_limit_bytes=VMEM_LIMIT),
    )(parts)


def sent_rows(experts):
    return -(-2 * experts * CAP // 16) * 16


def send_home(blocks, experts):
    sent = sent_rows(experts)
    far = exchanged(blocks[NX])
    near = [
        (
            block.astype(jnp.float32)
            + far[:, i * 2 * GROUP : (i + 1) * 2 * GROUP].astype(jnp.float32)
        ).astype(jnp.bfloat16)
        for i, block in enumerate(blocks[:NX])
    ]
    home = near[0].astype(jnp.float32)
    for block, step in zip(near[1:], STEPS, strict=True):
        home = home + shifted(block, "x", NX, NX - step).astype(jnp.float32)
    home = lax.dot_general(
        regroup_matrix(experts, sent),
        home.astype(jnp.bfloat16).reshape(experts * 2 * GROUP, D_PART),
        CONTRACT_ROWS,
        preferred_element_type=jnp.float32,
    ).astype(jnp.bfloat16)
    return swap(home.reshape(NY, sent, D_PART), "y").transpose(1, 0, 2).reshape(sent, D)


def per_device(tokens, expert_ids, gates, tile_slot, w_gate, w_up, w_down, grad_out):
    z_count = lax.axis_size("z")
    tok_rows = tokens.shape[0]
    experts = tile_slot.shape[0] // HTILES
    slot_count = experts * CAP
    sent = sent_rows(experts)
    slots = (tile_slot % z_count) * NX + tile_slot // z_count

    weight_parts = swap(weight_slices(w_gate, w_up, w_down), "x")
    weights = lax.all_gather(weight_parts, "z", axis=0, tiled=True)

    route_ids = expert_ids.reshape(-1)
    member = (route_ids[:, None] == jnp.arange(experts, dtype=jnp.int32)[None, :]).astype(jnp.int32)
    slot_rank = jnp.sum((jnp.cumsum(member, axis=0) - member) * member, axis=1)
    position = jnp.where(route_ids < experts, route_ids * CAP + slot_rank, slot_count)
    choose = (position[:, None] == jnp.arange(slot_count, dtype=jnp.int32)[None, :]).astype(
        jnp.float32
    )
    picker = jnp.sum(choose.reshape(tok_rows, TOPK, slot_count), axis=1)
    picker_half = picker.astype(jnp.bfloat16)
    gate_slot = jnp.dot(gates.reshape(-1), choose, precision=lax.Precision.HIGHEST)

    expert_rows = lax.dot_general(
        picker_half, tokens, CONTRACT_ROWS, preferred_element_type=jnp.float32
    ).astype(jnp.bfloat16)
    upstream = lax.dot_general(
        picker_half, grad_out, CONTRACT_ROWS, preferred_element_type=jnp.float32
    )
    scaled = (gate_slot[:, None] * upstream).astype(jnp.bfloat16)
    both = jnp.concatenate([expert_rows, scaled], axis=0)
    both = jnp.pad(both, ((0, sent - 2 * slot_count), (0, 0)))
    both = both.reshape(sent, NY, D_PART).transpose(1, 0, 2)
    regroup = regroup_matrix(experts, sent)
    own_rows = (
        jnp.dot(
            regroup,
            swap(both, "y").reshape(NY * sent, D_PART),
            preferred_element_type=jnp.float32,
        )
        .astype(jnp.bfloat16)
        .reshape(experts, 2 * GROUP, D_PART)
    )
    blocks = [own_rows] + [shifted(own_rows, "x", NX, step) for step in STEPS]
    rows = list(parted_rows(blocks, experts))
    rows = rows + [exchanged(block) for block in rows]

    partial = swap(partial_products(slots, weights, rows, experts), "y")
    pieces = partial.shape[0] // NY
    total = jnp.sum(partial.reshape(NY, pieces, 3 * PACKED, 128).astype(jnp.float32), axis=0)
    pre_gate, pre_up, hidden_grad = [
        total[:, matrix * PACKED : (matrix + 1) * PACKED] for matrix in range(3)
    ]
    sigmoid_gate = jax.nn.sigmoid(pre_gate)
    activated = pre_gate * sigmoid_gate
    acts = jnp.concatenate(
        [
            hidden_grad * pre_up * sigmoid_gate * (1.0 + pre_gate * (1.0 - sigmoid_gate)),
            hidden_grad * activated,
            activated * pre_up,
        ],
        axis=1,
    ).astype(jnp.bfloat16)
    acts = swap(jnp.tile(acts, (NY, 1, 1)), "y")

    grads = weight_grads(slots, acts, rows, experts, z_count * NX)
    grads, acts = lax.optimization_barrier((grads, acts))
    grads = swap(lax.psum_scatter(grads, "z", scatter_dimension=0, tiled=True), ("x", "c"))
    layer_out, gate_grads, token_grads = 0.0, 0.0, 0.0
    for first, count in PARTS:
        home = send_home(outputs(slots, weights, acts, first, count), count)
        here = slice(first * CAP, (first + count) * CAP)
        expert_out = home[: count * CAP].astype(jnp.float32)
        gated = (gate_slot[here, None] * expert_out).astype(jnp.bfloat16)
        layer_out += jnp.dot(picker_half[:, here], gated, preferred_element_type=jnp.float32)
        token_grads += jnp.dot(
            picker_half[:, here],
            home[count * CAP : 2 * count * CAP],
            preferred_element_type=jnp.float32,
        )
        gate_terms = jnp.sum(expert_out * upstream[here], axis=1)
        gate_grads += jnp.sum(choose[:, here] * gate_terms[None, :], axis=1)
    layer_out = layer_out.astype(jnp.bfloat16)
    token_grads = token_grads.astype(jnp.bfloat16)
    gate_grads = gate_grads.reshape(tok_rows, TOPK)
    grads, layer_out, token_grads, gate_grads = lax.optimization_barrier(
        (grads, layer_out, token_grads, gate_grads)
    )
    gate_weight_grads, up_weight_grads, down_weight_grads = tile_grads(grads)
    return (
        layer_out,
        token_grads,
        gate_grads,
        gate_weight_grads,
        up_weight_grads,
        down_weight_grads,
    )


def solution(mesh):
    dp, tile = ("y", "c"), ("x", "z")
    planes = Mesh(mesh.devices.reshape(NY, NC, NX, -1), dp + tile)
    rows = P(dp + tile, None)
    in_specs = (
        rows,
        rows,
        rows,
        P(),
        P(tile, None, None),
        P(tile, None, None),
        P(tile, None, None),
        rows,
    )
    out_specs = (
        rows,
        rows,
        rows,
        P(tile, dp, None),
        P(tile, dp, None),
        P(tile, None, dp),
    )
    return jax.shard_map(
        per_device, mesh=planes, in_specs=in_specs, out_specs=out_specs, check_vma=False
    )
```
